32 devices in a mesh: chan: 8 (over z, y), band: 4 (over x, core).
Axes of the slice: x: 2, y: 2, z: 4, core: 2. Of those that a mesh axis runs over, the one named last changes fastest.
Arguments:
- traces: bfloat16 [2048, 2, 4096], P('chan', None, 'band')
- row_ids: int32 [2048], P('chan'), may hold values from 0 to 2047, as said below
Outputs:
- cross: float32 [2, 64, 5, 8, 4096], P(None, 'chan', None, None, 'band')
The draws below stay inside these ranges and needn't reach their ends.
Inputs may be any that keep to these rules, and one draw needn't show every extreme that they name: Every channel-window number appears exactly once in row_ids. Of the rows held by one index of chan, at most 64 have row id // 256 equal to any one value, and that bound is reached.
All inputs are finite; a program needn't handle non-finite values.
Results may differ from the reference program's by a relative error of at most 0.003.
Values may be sent and summed in bfloat16 or wider, within the bound.
A program may use at most 64 MiB of HBM per device.

```python
import math
import jax
import jax.numpy as jnp
from jax import lax

F = 4096
WIN = 32
CH_DEV = 8
H = 2
CHANNELS = 64
ROWS = 2048
CAP = 64


def draw_traces(key, part):
    key_base, key_scale = jax.random.split(key, 2)
    ramp = 1.0 + 0.8 * jnp.arange(F, dtype=jnp.float32) / F
    base = jax.random.normal(key_base, (ROWS, 2, F), jnp.float32)
    row_scale = jnp.exp(jax.random.uniform(key_scale, (ROWS, 1, 1), jnp.float32) * math.log(10.0))
    return (base * ramp * row_scale).astype(jnp.bfloat16)


def draw_row_ids(key, part):
    n_devices = CHANNELS // CH_DEV
    per_device = CH_DEV * WIN
    key_pairs, key_perm, key_block, key_mix = jax.random.split(key, 4)
    halves = jax.random.randint(key_pairs, (n_devices // 2,), 0, CAP + 1).at[0].set(0)
    pattern = jnp.concatenate([halves, CAP - halves])[jax.random.permutation(key_perm, n_devices)]
    device_index = jnp.arange(n_devices)
    counts = pattern[(device_index[None, :] - device_index[:, None]) % n_devices]
    ends = jnp.cumsum(counts, axis=0)
    orders = jax.vmap(lambda subkey: jax.random.permutation(subkey, per_device))(jax.random.split(key_block, n_devices))
    identity = device_index[:, None] * per_device + orders
    positions = jnp.arange(per_device)
    sources = jnp.sum((positions[None, :, None] >= jnp.transpose(ends)[:, None, :]).astype(jnp.int32), axis=2)
    flat_ids = identity.reshape(-1)
    flat_sources = sources.reshape(-1)
    mixing = jax.random.permutation(key_mix, n_devices * per_device)
    ordering = jnp.argsort(flat_sources[mixing], stable=True)
    return flat_ids[mixing][ordering].astype(jnp.int32)


def setup_inputs(seed: int = 0) -> dict:
    seeds = jax.random.split(jax.random.key(seed), 3)
    traces = draw_traces(jax.random.fold_in(seeds[2], 71), 0)
    row_ids = draw_row_ids(jax.random.fold_in(seeds[2], 71), 0)
    return dict(traces=traces, row_ids=row_ids)


def reference(traces, row_ids):
    values = traces.astype(jnp.float32)
    power_mean = lax.optimization_barrier(jnp.sum(values * values, axis=(1, 2))) / F
    white = (values * (1.0 / jnp.sqrt(power_mean + 1e-06))[:, None, None]).astype(jnp.bfloat16)
    spectra = jnp.zeros((ROWS, 2, F), jnp.bfloat16).at[row_ids].set(white)
    block_count = CHANNELS // CH_DEV
    blocks = spectra.reshape(block_count, CH_DEV, WIN, 2, F)
    padding = jnp.zeros((H, CH_DEV, WIN, 2, F), jnp.bfloat16)
    padded = jnp.concatenate([padding, blocks, padding], axis=0)
    first_real = blocks[:, :, :, 0].astype(jnp.float32)
    first_imag = blocks[:, :, :, 1].astype(jnp.float32)
    outputs = []
    for offset in range(2 * H + 1):
        partner = padded[offset:offset + block_count]
        second_real = partner[:, :, :, 0].astype(jnp.float32)
        second_imag = partner[:, :, :, 1].astype(jnp.float32)
        real_part = (jnp.einsum('biwf,bjwf->bijf', first_real, second_real) + jnp.einsum('biwf,bjwf->bijf', first_imag, second_imag)) / WIN
        imag_part = (jnp.einsum('biwf,bjwf->bijf', first_imag, second_real) - jnp.einsum('biwf,bjwf->bijf', first_real, second_imag)) / WIN
        outputs.append(jnp.stack([real_part, imag_part]).reshape(2, CHANNELS, CH_DEV, F))
    return jnp.stack(outputs, axis=2)
```

```python
import functools

import jax
import jax.numpy as jnp
from jax import lax
from jax.experimental import pallas as pl
from jax.experimental.pallas import tpu as pltpu
from jax.sharding import PartitionSpec as P

F = 4096
WIN = 32
H = 2


def passed_along(block, axis, distance):
    devices = range(lax.axis_size(axis))
    route = [(i - distance, i) for i in devices if i - distance in devices]
    return lax.ppermute(block, axis, route)


def row_power(trace_rows):
    values = trace_rows.astype(jnp.float32)
    return jnp.sum(values * values, axis=1)


def scale_rows(trace_rows, power_total):
    factor = 1.0 / jnp.sqrt(power_total / F + 1e-06)
    return (trace_rows.astype(jnp.float32) * factor[:, None]).astype(jnp.bfloat16)


def spectra_pair(first, second):
    first_real = first[:, None, :, 0].astype(jnp.float32)
    first_imag = first[:, None, :, 1].astype(jnp.float32)
    second_real = second[None, :, :, 0].astype(jnp.float32)
    second_imag = second[None, :, :, 1].astype(jnp.float32)
    real_part = jnp.sum(first_real * second_real + first_imag * second_imag, axis=2)
    imag_part = jnp.sum(first_imag * second_real - first_real * second_imag, axis=2)
    return jnp.stack([real_part, imag_part]) / WIN


def body_by_rows(traces, row_ids):
    block_rows, _, band_bins = traces.shape
    trace_rows = traces.reshape(block_rows, 2 * band_bins)
    n_devices = lax.axis_size("chan")
    capacity = 2 * block_rows // n_devices
    trace_rows = scale_rows(trace_rows, lax.psum(row_power(trace_rows), "band"))
    owner_block = row_ids // block_rows
    member = (owner_block[:, None] == jnp.arange(n_devices)[None, :]).astype(jnp.int32)
    slot_rank = jnp.sum(member * (jnp.cumsum(member, axis=0) - 1), axis=1)
    slot_index = owner_block * capacity + slot_rank
    packing = slot_index[None, :] == jnp.arange(n_devices * capacity)[:, None]
    outgoing = jnp.dot(
        packing.astype(jnp.bfloat16), trace_rows, preferred_element_type=jnp.float32
    ).astype(jnp.bfloat16)
    label_values = (
        jnp.dot(
            packing.astype(jnp.float32),
            (row_ids + 1).astype(jnp.float32),
            precision=lax.Precision.HIGHEST,
        )
        - 1.0
    )
    sent_labels = label_values.astype(jnp.int32)
    arrived, arrived_ids = (
        lax.all_to_all(outgoing, "chan", split_axis=0, concat_axis=0, tiled=True),
        lax.all_to_all(sent_labels, "chan", split_axis=0, concat_axis=0, tiled=True),
    )
    placing = ((arrived_ids % block_rows)[None, :] == jnp.arange(block_rows)[:, None]) & (
        arrived_ids >= 0
    )[None, :]
    placed = jnp.dot(
        placing.astype(jnp.bfloat16), arrived, preferred_element_type=jnp.float32
    ).astype(jnp.bfloat16)
    chan_count = block_rows // WIN
    block_shape = (chan_count, WIN, 2, band_bins)
    local_block = placed.reshape(block_shape)
    spectra_list = [None] * (2 * H + 1)
    spectra_list[H] = spectra_pair(local_block, local_block)
    above_block = placed
    below_block = placed
    for offset in range(1, H + 1):
        above_block = passed_along(above_block, "chan", -1)
        spectra_list[H + offset] = spectra_pair(local_block, above_block.reshape(block_shape))
        below_block = passed_along(below_block, "chan", 1)
        spectra_list[H - offset] = spectra_pair(local_block, below_block.reshape(block_shape))
    return jnp.stack(spectra_list, axis=2)


LANES = 128
CH = 8
SLOTS = 2 * H + 1
MESH = pl.DeviceIdType.MESH


def exchange_kernel(n, xs_ref, pos_ref, o_ref, recv, placed, tmp, out, in_send, in_recv, out_send, out_recv):
    me = lax.axis_index("chan")
    rows = xs_ref.shape[1]

    barrier = pltpu.get_barrier_semaphore()
    for t in range(1, n):
        pl.semaphore_signal(
            barrier, inc=1, device_id={"chan": lax.rem(me + t, n)}, device_id_type=MESH
        )
    pl.semaphore_wait(barrier, n - 1)

    def row_copy(t):
        target = lax.rem(me + t, n)
        return pltpu.make_async_remote_copy(
            src_ref=xs_ref.at[target],
            dst_ref=recv.at[t],
            send_sem=in_send.at[t],
            recv_sem=in_recv.at[t],
            device_id={"chan": target},
            device_id_type=MESH,
        )

    order = sorted(range(1, n), key=lambda t: -min(t, n - t))
    for t in order:
        row_copy(t).start()

    def place(values, source, first):
        pos = pos_ref[pl.ds(source, 1), :]

        def chunk(b, carry):
            target = lax.broadcasted_iota(jnp.int32, (rows, rows), 0) + b * rows
            hot = jnp.where(pos == target, 1.0, 0.0).astype(jnp.bfloat16)
            part = jnp.dot(hot, values, preferred_element_type=jnp.float32)
            where = pl.ds(pl.multiple_of(b * rows, rows), rows)
            if first:
                placed[0, where, :] = part[:, :LANES]
                placed[1, where, :] = part[:, LANES:]
            else:
                placed[0, where, :] += part[:, :LANES]
                placed[1, where, :] += part[:, LANES:]
            return carry

        lax.fori_loop(0, n, chunk, 0)

    place(xs_ref[me], me, True)
    for t in reversed(order):
        row_copy(t).wait_recv()
        place(recv[t], lax.rem(me + n - t, n), False)

    def result_copy(dest, k):
        return pltpu.make_async_remote_copy(
            src_ref=out.at[dest, k],
            dst_ref=o_ref.at[me, k],
            send_sem=out_send.at[dest, k],
            recv_sem=out_recv.at[me, k],
            device_id={"chan": dest},
            device_id_type=MESH,
        )

    def deliver(dest, k):
        @pl.when(dest != me)
        def _():
            result_copy(dest, k).start()

        @pl.when(dest == me)
        def _():
            o_ref[me, k] = out[dest, k]

    def pair(d, offset):
        e = d + offset

        def window(w, acc):
            first = d * rows + w * CH
            second = pl.ds(pl.multiple_of(e * rows + w * CH, CH), CH)
            yr = placed[0, second, :]
            yi = placed[1, second, :]
            new = []
            for c in range(CH):
                xr = placed[0, pl.ds(first + c, 1), :]
                xi = placed[1, pl.ds(first + c, 1), :]
                re, im = acc[2 * c], acc[2 * c + 1]
                new.append(re + (xr * yr + xi * yi))
                new.append(im + (xi * yr - xr * yi))
            return tuple(new)

        zero = jnp.zeros((CH, LANES), jnp.float32)
        acc = lax.fori_loop(0, WIN, window, (zero,) * (2 * CH), unroll=4)
        for part in range(2):
            for c in range(CH):
                tmp[part, pl.ds(c * CH, CH), :] = acc[2 * c + part] * (1.0 / WIN)
        for part in range(2):
            out[d, H + offset, part] = tmp[part].astype(jnp.bfloat16)
        deliver(d, H + offset)
        if offset:
            for part in range(2):
                turned = jnp.concatenate(
                    [tmp[part, pl.ds(c, CH, stride=CH), :] for c in range(CH)], axis=0
                )
                turned = turned if part == 0 else -turned
                out[e, H - offset, part] = turned.astype(jnp.bfloat16)
            deliver(e, H - offset)

    def block_step(t, carry):
        d = lax.rem(me + n // 2 + t, n)
        pair(d, 0)
        for offset in range(1, H + 1):
            pl.when(d + offset < n)(functools.partial(pair, d, offset))
        return carry

    lax.fori_loop(0, n, block_step, 0)

    for k in range(SLOTS):
        partner = me + k - H

        @pl.when((partner < 0) | (partner >= n))
        def _():
            for source in range(n):
                o_ref[source, k] = jnp.zeros(o_ref.shape[2:], o_ref.dtype)

    for t in range(1, n):
        row_copy(t).wait_send()
        dest = lax.rem(me + t, n)
        source = lax.rem(me + n - t, n)
        for k in range(SLOTS):
            there = dest + k - H
            here = me + k - H

            @pl.when((there >= 0) & (there < n))
            def _():
                result_copy(dest, k).wait_send()

            @pl.when((here >= 0) & (here < n))
            def _():
                pltpu.make_async_remote_copy(
                    src_ref=out.at[source, k],
                    dst_ref=o_ref.at[source, k],
                    send_sem=out_send.at[source, k],
                    recv_sem=out_recv.at[source, k],
                    device_id={"chan": source},
                    device_id_type=MESH,
                ).wait_recv()


def unpack_kernel(n, in_ref, out_ref):
    for source in range(n):
        for k in range(SLOTS):
            values = in_ref[source, k, 0].astype(jnp.float32)
            for c in range(CH):
                out_ref[0, c, k, :, source * LANES : (source + 1) * LANES] = values[c * CH : (c + 1) * CH]


def body_by_bins(traces, row_ids):
    rows, _, band_bins = traces.shape
    n = lax.axis_size("chan")
    flat = traces.reshape(rows, 2 * band_bins)
    white = scale_rows(flat, lax.psum(row_power(flat), "band"))
    xs = white.reshape(rows, 2, n, LANES).transpose(2, 0, 1, 3).reshape(n, rows, 2 * LANES)
    ids = lax.all_gather(row_ids, "chan")
    pos = (ids // rows) * rows + (ids % WIN) * CH + (ids // WIN) % CH
    vmem = pl.BlockSpec(memory_space=pltpu.VMEM)
    packed = pl.pallas_call(
        functools.partial(exchange_kernel, n),
        out_shape=jax.ShapeDtypeStruct((n, SLOTS, 2, CH * CH, LANES), jnp.bfloat16),
        in_specs=[vmem, vmem],
        out_specs=vmem,
        scratch_shapes=[
            pltpu.VMEM((n, rows, 2 * LANES), jnp.bfloat16),
            pltpu.VMEM((2, n * rows, LANES), jnp.float32),
            pltpu.VMEM((2, CH * CH, LANES), jnp.float32),
            pltpu.VMEM((n, SLOTS, 2, CH * CH, LANES), jnp.bfloat16),
            pltpu.SemaphoreType.DMA((n,)),
            pltpu.SemaphoreType.DMA((n,)),
            pltpu.SemaphoreType.DMA((n, SLOTS)),
            pltpu.SemaphoreType.DMA((n, SLOTS)),
        ],
        compiler_params=pltpu.CompilerParams(
            collective_id=0, has_side_effects=True, vmem_limit_bytes=40 * 2**20
        ),
    )(xs, pos)
    return pl.pallas_call(
        functools.partial(unpack_kernel, n),
        grid=(2,),
        out_shape=jax.ShapeDtypeStruct((2, rows // WIN, SLOTS, CH, band_bins), jnp.float32),
        in_specs=[pl.BlockSpec((n, SLOTS, 1, CH * CH, LANES), lambda p: (0, 0, p, 0, 0))],
        out_specs=pl.BlockSpec((1, rows // WIN, SLOTS, CH, band_bins), lambda p: (p, 0, 0, 0, 0)),
        compiler_params=pltpu.CompilerParams(vmem_limit_bytes=40 * 2**20),
    )(packed)


def body(traces, row_ids):
    rows, _, band_bins = traces.shape
    by_bins = band_bins == lax.axis_size("chan") * LANES and rows == CH * WIN
    return (body_by_bins if by_bins else body_by_rows)(traces, row_ids)


def solution(mesh):
    in_specs = (P("chan", None, "band"), P("chan"))
    out_specs = P(None, "chan", None, None, "band")
    return jax.shard_map(body, mesh=mesh, in_specs=in_specs, out_specs=out_specs, check_vma=False)
```

```python
import functools

import jax
import jax.numpy as jnp
from jax import lax
from jax.experimental import pallas as pl
from jax.experimental.pallas import tpu as pltpu
from jax.sharding import PartitionSpec as P

F = 4096
WIN = 32
H = 2


def passed_along(block, axis, distance):
    devices = range(lax.axis_size(axis))
    route = [(i - distance, i) for i in devices if i - distance in devices]
    return lax.ppermute(block, axis, route)


def row_power(trace_rows):
    values = trace_rows.astype(jnp.float32)
    return jnp.sum(values * values, axis=1)


def scale_rows(trace_rows, power_total):
    factor = 1.0 / jnp.sqrt(power_total / F + 1e-06)
    return (trace_rows.astype(jnp.float32) * factor[:, None]).astype(jnp.bfloat16)


def spectra_pair(first, second):
    first_real = first[:, None, :, 0].astype(jnp.float32)
    first_imag = first[:, None, :, 1].astype(jnp.float32)
    second_real = second[None, :, :, 0].astype(jnp.float32)
    second_imag = second[None, :, :, 1].astype(jnp.float32)
    real_part = jnp.sum(first_real * second_real + first_imag * second_imag, axis=2)
    imag_part = jnp.sum(first_imag * second_real - first_real * second_imag, axis=2)
    return jnp.stack([real_part, imag_part]) / WIN


def body_by_rows(traces, row_ids):
    block_rows, _, band_bins = traces.shape
    trace_rows = traces.reshape(block_rows, 2 * band_bins)
    n_devices = lax.axis_size("chan")
    capacity = 2 * block_rows // n_devices
    trace_rows = scale_rows(trace_rows, lax.psum(row_power(trace_rows), "band"))
    owner_block = row_ids // block_rows
    member = (owner_block[:, None] == jnp.arange(n_devices)[None, :]).astype(jnp.int32)
    slot_rank = jnp.sum(member * (jnp.cumsum(member, axis=0) - 1), axis=1)
    slot_index = owner_block * capacity + slot_rank
    packing = slot_index[None, :] == jnp.arange(n_devices * capacity)[:, None]
    outgoing = jnp.dot(
        packing.astype(jnp.bfloat16), trace_rows, preferred_element_type=jnp.float32
    ).astype(jnp.bfloat16)
    label_values = (
        jnp.dot(
            packing.astype(jnp.float32),
            (row_ids + 1).astype(jnp.float32),
            precision=lax.Precision.HIGHEST,
        )
        - 1.0
    )
    sent_labels = label_values.astype(jnp.int32)
    arrived, arrived_ids = (
        lax.all_to_all(outgoing, "chan", split_axis=0, concat_axis=0, tiled=True),
        lax.all_to_all(sent_labels, "chan", split_axis=0, concat_axis=0, tiled=True),
    )
    placing = ((arrived_ids % block_rows)[None, :] == jnp.arange(block_rows)[:, None]) & (
        arrived_ids >= 0
    )[None, :]
    placed = jnp.dot(
        placing.astype(jnp.bfloat16), arrived, preferred_element_type=jnp.float32
    ).astype(jnp.bfloat16)
    chan_count = block_rows // WIN
    block_shape = (chan_count, WIN, 2, band_bins)
    local_block = placed.reshape(block_shape)
    spectra_list = [None] * (2 * H + 1)
    spectra_list[H] = spectra_pair(local_block, local_block)
    above_block = placed
    below_block = placed
    for offset in range(1, H + 1):
        above_block = passed_along(above_block, "chan", -1)
        spectra_list[H + offset] = spectra_pair(local_block, above_block.reshape(block_shape))
        below_block = passed_along(below_block, "chan", 1)
        spectra_list[H - offset] = spectra_pair(local_block, below_block.reshape(block_shape))
    return jnp.stack(spectra_list, axis=2)


LANES = 128
CH = 8
SLOTS = 2 * H + 1
MESH = pl.DeviceIdType.MESH


def exchange_kernel(
    n, nb, flat_ref, pos_ref, o_ref, recv, placed, tmp, out, power, powers, label, labels,
    in_send, in_recv, out_send, out_recv, power_send, power_recv, label_send, label_recv,
):
    me = lax.axis_index("chan")
    mine = lax.axis_index("band")
    rows, width = flat_ref.shape
    band_bins = width // 2

    barrier = pltpu.get_barrier_semaphore()
    for t in range(1, n):
        pl.semaphore_signal(
            barrier, inc=1, device_id={"chan": lax.rem(me + t, n)}, device_id_type=MESH
        )
    for t in range(1, nb):
        pl.semaphore_signal(
            barrier, inc=1, device_id={"band": lax.rem(mine + t, nb)}, device_id_type=MESH
        )

    total = jnp.zeros((rows, LANES), jnp.float32)
    for i in range(width // LANES):
        value = flat_ref[:, i * LANES : (i + 1) * LANES].astype(jnp.float32)
        total += value * value
    ones = jnp.ones((8, LANES), jnp.bfloat16)
    row_sum = jnp.zeros((8, rows), jnp.float32)
    for _ in range(3):
        term = total.astype(jnp.bfloat16)
        total -= term.astype(jnp.float32)
        row_sum += lax.dot_general(
            ones, term, (((1,), (1,)), ((), ())), preferred_element_type=jnp.float32
        )
    power[...] = row_sum

    pl.semaphore_wait(barrier, n - 1 + nb - 1)

    def power_copy(t):
        return pltpu.make_async_remote_copy(
            src_ref=power,
            dst_ref=powers.at[t],
            send_sem=power_send.at[t],
            recv_sem=power_recv.at[t],
            device_id={"band": lax.rem(mine + t, nb)},
            device_id_type=MESH,
        )

    def label_copy(t):
        return pltpu.make_async_remote_copy(
            src_ref=label,
            dst_ref=labels.at[t],
            send_sem=label_send.at[t],
            recv_sem=label_recv.at[t],
            device_id={"chan": lax.rem(me + t, n)},
            device_id_type=MESH,
        )

    def row_copy(t, part):
        target = lax.rem(me + t, n)
        bins = pl.multiple_of(part * band_bins + target * LANES, LANES)
        return pltpu.make_async_remote_copy(
            src_ref=flat_ref.at[:, pl.ds(bins, LANES)],
            dst_ref=recv.at[t, part],
            send_sem=in_send.at[t, part],
            recv_sem=in_recv.at[t, part],
            device_id={"chan": target},
            device_id_type=MESH,
        )

    for t in range(1, nb):
        power_copy(t).start()
    order = sorted(range(1, n), key=lambda t: -min(t, n - t))
    for t in order:
        for part in range(2):
            row_copy(t, part).start()

    power_total = power[...]
    for t in range(1, nb):
        power_copy(t).wait_recv()
        power_total += powers[t]
    label[:8] = 1.0 / jnp.sqrt(power_total / F + 1e-06)
    label[8:] = pos_ref[...].astype(jnp.float32)
    for t in range(1, n):
        label_copy(t).start()

    def place(parts, held, first):
        factor = jnp.transpose(held[:8])[:, :1]
        pos = held[8:9].astype(jnp.int32)
        values = jnp.concatenate(
            [(x.astype(jnp.float32) * factor).astype(jnp.bfloat16) for x in parts], axis=1
        )

        def chunk(b, carry):
            target = lax.broadcasted_iota(jnp.int32, (rows, rows), 0) + b * rows
            hot = jnp.where(pos == target, 1.0, 0.0).astype(jnp.bfloat16)
            product = jnp.dot(hot, values, preferred_element_type=jnp.float32)
            where = pl.ds(pl.multiple_of(b * rows, rows), rows)
            for part in range(2):
                term = product[:, part * LANES : (part + 1) * LANES]
                placed[part, where, :] = term if first else placed[part, where, :] + term
            return carry

        lax.fori_loop(0, n, chunk, 0)

    own = [
        flat_ref[:, pl.ds(pl.multiple_of(part * band_bins + me * LANES, LANES), LANES)]
        for part in range(2)
    ]
    place(own, label[...], True)
    for t in reversed(order):
        label_copy(t).wait_recv()
        for part in range(2):
            row_copy(t, part).wait_recv()
        place([recv[t, 0], recv[t, 1]], labels[t], False)

    def result_copy(dest, k):
        return pltpu.make_async_remote_copy(
            src_ref=out.at[dest, k],
            dst_ref=o_ref.at[me, k],
            send_sem=out_send.at[dest, k],
            recv_sem=out_recv.at[me, k],
            device_id={"chan": dest},
            device_id_type=MESH,
        )

    def deliver(dest, k):
        @pl.when(dest != me)
        def _():
            result_copy(dest, k).start()

        @pl.when(dest == me)
        def _():
            o_ref[me, k] = out[dest, k]

    def pair(d, offset):
        e = d + offset

        def window(w, acc):
            first = d * rows + w * CH
            second = pl.ds(pl.multiple_of(e * rows + w * CH, CH), CH)
            yr = placed[0, second, :]
            yi = placed[1, second, :]
            new = []
            for c in range(CH):
                xr = placed[0, pl.ds(first + c, 1), :]
                xi = placed[1, pl.ds(first + c, 1), :]
                re, im = acc[2 * c], acc[2 * c + 1]
                new.append(re + (xr * yr + xi * yi))
                new.append(im + (xi * yr - xr * yi))
            return tuple(new)

        zero = jnp.zeros((CH, LANES), jnp.float32)
        acc = lax.fori_loop(0, WIN, window, (zero,) * (2 * CH), unroll=4)
        for part in range(2):
            for c in range(CH):
                tmp[part, pl.ds(c * CH, CH), :] = acc[2 * c + part] * (1.0 / WIN)
        for part in range(2):
            out[d, H + offset, part] = tmp[part].astype(jnp.bfloat16)
        deliver(d, H + offset)
        if offset:
            for part in range(2):
                turned = jnp.concatenate(
                    [tmp[part, pl.ds(c, CH, stride=CH), :] for c in range(CH)], axis=0
                )
                turned = turned if part == 0 else -turned
                out[e, H - offset, part] = turned.astype(jnp.bfloat16)
            deliver(e, H - offset)

    def block_step(t, carry):
        d = lax.rem(me + n // 2 + t, n)
        pair(d, 0)
        for offset in range(1, H + 1):
            pl.when(d + offset < n)(functools.partial(pair, d, offset))
        return carry

    lax.fori_loop(0, n, block_step, 0)

    for k in range(SLOTS):
        partner = me + k - H

        @pl.when((partner < 0) | (partner >= n))
        def _():
            for source in range(n):
                o_ref[source, k] = jnp.zeros(o_ref.shape[2:], o_ref.dtype)

    for t in range(1, nb):
        power_copy(t).wait_send()
    for t in range(1, n):
        label_copy(t).wait_send()
        for part in range(2):
            row_copy(t, part).wait_send()
        dest = lax.rem(me + t, n)
        source = lax.rem(me + n - t, n)
        for k in range(SLOTS):
            there = dest + k - H
            here = me + k - H

            @pl.when((there >= 0) & (there < n))
            def _():
                result_copy(dest, k).wait_send()

            @pl.when((here >= 0) & (here < n))
            def _():
                pltpu.make_async_remote_copy(
                    src_ref=out.at[source, k],
                    dst_ref=o_ref.at[source, k],
                    send_sem=out_send.at[source, k],
                    recv_sem=out_recv.at[source, k],
                    device_id={"chan": source},
                    device_id_type=MESH,
                ).wait_recv()


def unpack_kernel(n, in_ref, out_ref):
    for source in range(n):
        for k in range(SLOTS):
            values = in_ref[source, k, 0].astype(jnp.float32)
            for c in range(CH):
                out_ref[0, c, k, :, source * LANES : (source + 1) * LANES] = values[c * CH : (c + 1) * CH]


def body_by_bins(traces, row_ids):
    rows, _, band_bins = traces.shape
    n = lax.axis_size("chan")
    nb = lax.axis_size("band")
    flat = traces.reshape(rows, 2 * band_bins)
    pos = (row_ids // rows) * rows + (row_ids % WIN) * CH + (row_ids // WIN) % CH
    pos = jnp.broadcast_to(pos[None, :], (8, rows))
    vmem = pl.BlockSpec(memory_space=pltpu.VMEM)
    packed = pl.pallas_call(
        functools.partial(exchange_kernel, n, nb),
        out_shape=jax.ShapeDtypeStruct((n, SLOTS, 2, CH * CH, LANES), jnp.bfloat16),
        in_specs=[vmem, vmem],
        out_specs=vmem,
        scratch_shapes=[
            pltpu.VMEM((n, 2, rows, LANES), jnp.bfloat16),
            pltpu.VMEM((2, n * rows, LANES), jnp.float32),
            pltpu.VMEM((2, CH * CH, LANES), jnp.float32),
            pltpu.VMEM((n, SLOTS, 2, CH * CH, LANES), jnp.bfloat16),
            pltpu.VMEM((8, rows), jnp.float32),
            pltpu.VMEM((nb, 8, rows), jnp.float32),
            pltpu.VMEM((16, rows), jnp.float32),
            pltpu.VMEM((n, 16, rows), jnp.float32),
            pltpu.SemaphoreType.DMA((n, 2)),
            pltpu.SemaphoreType.DMA((n, 2)),
            pltpu.SemaphoreType.DMA((n, SLOTS)),
            pltpu.SemaphoreType.DMA((n, SLOTS)),
            pltpu.SemaphoreType.DMA((nb,)),
            pltpu.SemaphoreType.DMA((nb,)),
            pltpu.SemaphoreType.DMA((n,)),
            pltpu.SemaphoreType.DMA((n,)),
        ],
        compiler_params=pltpu.CompilerParams(
            collective_id=0, has_side_effects=True, vmem_limit_bytes=40 * 2**20
        ),
    )(flat, pos)
    return pl.pallas_call(
        functools.partial(unpack_kernel, n),
        grid=(2,),
        out_shape=jax.ShapeDtypeStruct((2, rows // WIN, SLOTS, CH, band_bins), jnp.float32),
        in_specs=[pl.BlockSpec((n, SLOTS, 1, CH * CH, LANES), lambda p: (0, 0, p, 0, 0))],
        out_specs=pl.BlockSpec((1, rows // WIN, SLOTS, CH, band_bins), lambda p: (p, 0, 0, 0, 0)),
        compiler_params=pltpu.CompilerParams(vmem_limit_bytes=40 * 2**20),
    )(packed)


def body(traces, row_ids):
    rows, _, band_bins = traces.shape
    by_bins = band_bins == lax.axis_size("chan") * LANES and rows == CH * WIN
    return (body_by_bins if by_bins else body_by_rows)(traces, row_ids)


def solution(mesh):
    in_specs = (P("chan", None, "band"), P("chan"))
    out_specs = P(None, "chan", None, None, "band")
    return jax.shard_map(body, mesh=mesh, in_specs=in_specs, out_specs=out_specs, check_vma=False)
```

```python
import functools

import jax
import jax.numpy as jnp
from jax import lax
from jax.experimental import pallas as pl
from jax.experimental.pallas import tpu as pltpu
from jax.sharding import PartitionSpec as P

F = 4096
WIN = 32
H = 2


def passed_along(block, axis, distance):
    devices = range(lax.axis_size(axis))
    route = [(i - distance, i) for i in devices if i - distance in devices]
    return lax.ppermute(block, axis, route)


def row_power(trace_rows):
    values = trace_rows.astype(jnp.float32)
    return jnp.sum(values * values, axis=1)


def scale_rows(trace_rows, power_total):
    factor = 1.0 / jnp.sqrt(power_total / F + 1e-06)
    return (trace_rows.astype(jnp.float32) * factor[:, None]).astype(jnp.bfloat16)


def spectra_pair(first, second):
    first_real = first[:, None, :, 0].astype(jnp.float32)
    first_imag = first[:, None, :, 1].astype(jnp.float32)
    second_real = second[None, :, :, 0].astype(jnp.float32)
    second_imag = second[None, :, :, 1].astype(jnp.float32)
    real_part = jnp.sum(first_real * second_real + first_imag * second_imag, axis=2)
    imag_part = jnp.sum(first_imag * second_real - first_real * second_imag, axis=2)
    return jnp.stack([real_part, imag_part]) / WIN


def body_by_rows(traces, row_ids):
    block_rows, _, band_bins = traces.shape
    trace_rows = traces.reshape(block_rows, 2 * band_bins)
    n_devices = lax.axis_size("chan")
    capacity = 2 * block_rows // n_devices
    trace_rows = scale_rows(trace_rows, lax.psum(row_power(trace_rows), "band"))
    owner_block = row_ids // block_rows
    member = (owner_block[:, None] == jnp.arange(n_devices)[None, :]).astype(jnp.int32)
    slot_rank = jnp.sum(member * (jnp.cumsum(member, axis=0) - 1), axis=1)
    slot_index = owner_block * capacity + slot_rank
    packing = slot_index[None, :] == jnp.arange(n_devices * capacity)[:, None]
    outgoing = jnp.dot(
        packing.astype(jnp.bfloat16), trace_rows, preferred_element_type=jnp.float32
    ).astype(jnp.bfloat16)
    label_values = (
        jnp.dot(
            packing.astype(jnp.float32),
            (row_ids + 1).astype(jnp.float32),
            precision=lax.Precision.HIGHEST,
        )
        - 1.0
    )
    sent_labels = label_values.astype(jnp.int32)
    arrived, arrived_ids = (
        lax.all_to_all(outgoing, "chan", split_axis=0, concat_axis=0, tiled=True),
        lax.all_to_all(sent_labels, "chan", split_axis=0, concat_axis=0, tiled=True),
    )
    placing = ((arrived_ids % block_rows)[None, :] == jnp.arange(block_rows)[:, None]) & (
        arrived_ids >= 0
    )[None, :]
    placed = jnp.dot(
        placing.astype(jnp.bfloat16), arrived, preferred_element_type=jnp.float32
    ).astype(jnp.bfloat16)
    chan_count = block_rows // WIN
    block_shape = (chan_count, WIN, 2, band_bins)
    local_block = placed.reshape(block_shape)
    spectra_list = [None] * (2 * H + 1)
    spectra_list[H] = spectra_pair(local_block, local_block)
    above_block = placed
    below_block = placed
    for offset in range(1, H + 1):
        above_block = passed_along(above_block, "chan", -1)
        spectra_list[H + offset] = spectra_pair(local_block, above_block.reshape(block_shape))
        below_block = passed_along(below_block, "chan", 1)
        spectra_list[H - offset] = spectra_pair(local_block, below_block.reshape(block_shape))
    return jnp.stack(spectra_list, axis=2)


LANES = 128
CH = 8
SLOTS = 2 * H + 1
MESH = pl.DeviceIdType.MESH


def exchange_kernel(
    n, nb, flat_ref, ids_ref, o_ref, recv, hot, white, placed, tmp, out, power, powers, labels,
    in_send, in_recv, out_send, out_recv, power_send, power_recv, label_send, label_recv,
):
    me = lax.axis_index("chan")
    mine = lax.axis_index("band")
    rows, width = flat_ref.shape
    band_bins = width // 2

    barrier = pltpu.get_barrier_semaphore()
    for t in range(1, n):
        pl.semaphore_signal(
            barrier, inc=1, device_id={"chan": lax.rem(me + t, n)}, device_id_type=MESH
        )
    for t in range(1, nb):
        pl.semaphore_signal(
            barrier, inc=1, device_id={"band": lax.rem(mine + t, nb)}, device_id_type=MESH
        )

    total = jnp.zeros((rows, LANES), jnp.float32)
    for i in range(width // LANES):
        value = flat_ref[:, i * LANES : (i + 1) * LANES].astype(jnp.float32)
        total += value * value
    ones = jnp.ones((8, LANES), jnp.bfloat16)
    row_sum = jnp.zeros((8, rows), jnp.float32)
    for _ in range(3):
        term = total.astype(jnp.bfloat16)
        total -= term.astype(jnp.float32)
        row_sum += lax.dot_general(
            ones, term, (((1,), (1,)), ((), ())), preferred_element_type=jnp.float32
        )
    ids = ids_ref[...]
    inside = ids & (rows - 1)
    pos = ids - inside + (ids & (WIN - 1)) * CH + lax.shift_right_logical(inside, WIN.bit_length() - 1)
    pos = jnp.broadcast_to(pos, (8, rows)).astype(jnp.float32)
    upper = lax.broadcasted_iota(jnp.int32, (8, rows), 0) < 4
    labels[0] = jnp.where(upper, row_sum, pos)

    pl.semaphore_wait(barrier, n - 1 + nb - 1)

    def power_copy(t):
        return pltpu.make_async_remote_copy(
            src_ref=power,
            dst_ref=powers.at[t],
            send_sem=power_send.at[t],
            recv_sem=power_recv.at[t],
            device_id={"band": lax.rem(mine + t, nb)},
            device_id_type=MESH,
        )

    def label_copy(t):
        return pltpu.make_async_remote_copy(
            src_ref=labels.at[0],
            dst_ref=labels.at[t],
            send_sem=label_send.at[t],
            recv_sem=label_recv.at[t],
            device_id={"chan": lax.rem(me + t, n)},
            device_id_type=MESH,
        )

    def row_copy(t, part):
        target = lax.rem(me + t, n)
        bins = pl.multiple_of(part * band_bins + target * LANES, LANES)
        return pltpu.make_async_remote_copy(
            src_ref=flat_ref.at[:, pl.ds(bins, LANES)],
            dst_ref=recv.at[t, part],
            send_sem=in_send.at[t, part],
            recv_sem=in_recv.at[t, part],
            device_id={"chan": target},
            device_id_type=MESH,
        )

    order = sorted(range(1, n), key=lambda t: -min(t, n - t))
    for t in order:
        label_copy(t).start()
    for t in order:
        for part in range(2):
            row_copy(t, part).start()

    power[0:1] = labels[0, 0:1]
    for t in reversed(order):
        label_copy(t).wait_recv()
        power[t : t + 1] = labels[t, 0:1]
    for t in range(1, nb):
        power_copy(t).start()

    def hot_chunk(b, carry):
        target = lax.broadcasted_iota(jnp.int32, (rows, rows), 0) + b * rows
        where = pl.ds(pl.multiple_of(b * rows, rows), rows)
        for t in range(n):
            place = labels[t, 4:5].astype(jnp.int32)
            hot[where, t * rows : (t + 1) * rows] = jnp.where(
                place == target, 1.0, 0.0
            ).astype(jnp.bfloat16)
        return carry

    lax.fori_loop(0, n, hot_chunk, 0)

    power_total = power[...]
    for t in range(1, nb):
        power_copy(t).wait_recv()
        power_total += powers[t]
    factor = jnp.transpose(1.0 / jnp.sqrt(power_total / F + 1e-06))

    def whiten(t, parts):
        for part in range(2):
            value = parts[part].astype(jnp.float32) * factor[:, t : t + 1]
            white[t * rows : (t + 1) * rows, part * LANES : (part + 1) * LANES] = value.astype(
                jnp.bfloat16
            )

    whiten(
        0,
        [
            flat_ref[:, pl.ds(pl.multiple_of(part * band_bins + me * LANES, LANES), LANES)]
            for part in range(2)
        ],
    )
    for t in reversed(order):
        for part in range(2):
            row_copy(t, part).wait_recv()
        whiten(t, [recv[t, 0], recv[t, 1]])

    def place_chunk(b, carry):
        where = pl.ds(pl.multiple_of(b * rows, rows), rows)
        product = jnp.dot(hot[where, :], white[...], preferred_element_type=jnp.float32)
        placed[0, where, :] = product[:, :LANES]
        placed[1, where, :] = product[:, LANES:]
        return carry

    lax.fori_loop(0, n, place_chunk, 0)

    def result_copy(dest, k):
        return pltpu.make_async_remote_copy(
            src_ref=out.at[dest, k],
            dst_ref=o_ref.at[me, k],
            send_sem=out_send.at[dest, k],
            recv_sem=out_recv.at[me, k],
            device_id={"chan": dest},
            device_id_type=MESH,
        )

    def deliver(dest, k):
        @pl.when(dest != me)
        def _():
            result_copy(dest, k).start()

        @pl.when(dest == me)
        def _():
            o_ref[me, k] = out[dest, k]

    def pair(d, offset):
        e = d + offset

        def window(w, acc):
            first = d * rows + w * CH
            second = pl.ds(pl.multiple_of(e * rows + w * CH, CH), CH)
            yr = placed[0, second, :]
            yi = placed[1, second, :]
            new = []
            for c in range(CH):
                xr = placed[0, pl.ds(first + c, 1), :]
                xi = placed[1, pl.ds(first + c, 1), :]
                re, im = acc[2 * c], acc[2 * c + 1]
                new.append(re + (xr * yr + xi * yi))
                new.append(im + (xi * yr - xr * yi))
            return tuple(new)

        zero = jnp.zeros((CH, LANES), jnp.float32)
        acc = lax.fori_loop(0, WIN, window, (zero,) * (2 * CH), unroll=4)
        for part in range(2):
            for c in range(CH):
                tmp[part, pl.ds(c * CH, CH), :] = acc[2 * c + part] * (1.0 / WIN)
        for part in range(2):
            out[d, H + offset, part] = tmp[part].astype(jnp.bfloat16)
        deliver(d, H + offset)
        if offset:
            for part in range(2):
                turned = jnp.concatenate(
                    [tmp[part, pl.ds(c, CH, stride=CH), :] for c in range(CH)], axis=0
                )
                turned = turned if part == 0 else -turned
                out[e, H - offset, part] = turned.astype(jnp.bfloat16)
            deliver(e, H - offset)

    def block_step(t, carry):
        d = lax.rem(me + n // 2 + t, n)
        pair(d, 0)
        for offset in range(1, H + 1):
            pl.when(d + offset < n)(functools.partial(pair, d, offset))
        return carry

    lax.fori_loop(0, n, block_step, 0)

    for k in range(SLOTS):
        partner = me + k - H

        @pl.when((partner < 0) | (partner >= n))
        def _():
            for source in range(n):
                o_ref[source, k] = jnp.zeros(o_ref.shape[2:], o_ref.dtype)

    for t in range(1, nb):
        power_copy(t).wait_send()
    for t in range(1, n):
        label_copy(t).wait_send()
        for part in range(2):
            row_copy(t, part).wait_send()
        dest = lax.rem(me + t, n)
        source = lax.rem(me + n - t, n)
        for k in range(SLOTS):
            there = dest + k - H
            here = me + k - H

            @pl.when((there >= 0) & (there < n))
            def _():
                result_copy(dest, k).wait_send()

            @pl.when((here >= 0) & (here < n))
            def _():
                pltpu.make_async_remote_copy(
                    src_ref=out.at[source, k],
                    dst_ref=o_ref.at[source, k],
                    send_sem=out_send.at[source, k],
                    recv_sem=out_recv.at[source, k],
                    device_id={"chan": source},
                    device_id_type=MESH,
                ).wait_recv()


def unpack_kernel(n, in_ref, out_ref):
    for source in range(n):
        for k in range(SLOTS):
            values = in_ref[source, k, 0].astype(jnp.float32)
            for c in range(CH):
                out_ref[0, c, k, :, source * LANES : (source + 1) * LANES] = values[c * CH : (c + 1) * CH]


def body_by_bins(traces, row_ids):
    rows, _, band_bins = traces.shape
    n = lax.axis_size("chan")
    nb = lax.axis_size("band")
    flat = traces.reshape(rows, 2 * band_bins)
    vmem = pl.BlockSpec(memory_space=pltpu.VMEM)
    packed = pl.pallas_call(
        functools.partial(exchange_kernel, n, nb),
        out_shape=jax.ShapeDtypeStruct((n, SLOTS, 2, CH * CH, LANES), jnp.bfloat16),
        in_specs=[vmem, vmem],
        out_specs=vmem,
        scratch_shapes=[
            pltpu.VMEM((n, 2, rows, LANES), jnp.bfloat16),
            pltpu.VMEM((n * rows, n * rows), jnp.bfloat16),
            pltpu.VMEM((n * rows, 2 * LANES), jnp.bfloat16),
            pltpu.VMEM((2, n * rows, LANES), jnp.float32),
            pltpu.VMEM((2, CH * CH, LANES), jnp.float32),
            pltpu.VMEM((n, SLOTS, 2, CH * CH, LANES), jnp.bfloat16),
            pltpu.VMEM((n, rows), jnp.float32),
            pltpu.VMEM((nb, n, rows), jnp.float32),
            pltpu.VMEM((n, 8, rows), jnp.float32),
            pltpu.SemaphoreType.DMA((n, 2)),
            pltpu.SemaphoreType.DMA((n, 2)),
            pltpu.SemaphoreType.DMA((n, SLOTS)),
            pltpu.SemaphoreType.DMA((n, SLOTS)),
            pltpu.SemaphoreType.DMA((nb,)),
            pltpu.SemaphoreType.DMA((nb,)),
            pltpu.SemaphoreType.DMA((n,)),
            pltpu.SemaphoreType.DMA((n,)),
        ],
        compiler_params=pltpu.CompilerParams(
            collective_id=0, has_side_effects=True, vmem_limit_bytes=40 * 2**20
        ),
    )(flat, row_ids.reshape(1, rows))
    return pl.pallas_call(
        functools.partial(unpack_kernel, n),
        grid=(2,),
        out_shape=jax.ShapeDtypeStruct((2, rows // WIN, SLOTS, CH, band_bins), jnp.float32),
        in_specs=[pl.BlockSpec((n, SLOTS, 1, CH * CH, LANES), lambda p: (0, 0, p, 0, 0))],
        out_specs=pl.BlockSpec((1, rows // WIN, SLOTS, CH, band_bins), lambda p: (p, 0, 0, 0, 0)),
        compiler_params=pltpu.CompilerParams(vmem_limit_bytes=40 * 2**20),
    )(packed)


def body(traces, row_ids):
    rows, _, band_bins = traces.shape
    by_bins = band_bins == lax.axis_size("chan") * LANES and rows == CH * WIN
    return (body_by_bins if by_bins else body_by_rows)(traces, row_ids)


def solution(mesh):
    in_specs = (P("chan", None, "band"), P("chan"))
    out_specs = P(None, "chan", None, None, "band")
    return jax.shard_map(body, mesh=mesh, in_specs=in_specs, out_specs=out_specs, check_vma=False)
```

```python
import functools

import jax
import jax.numpy as jnp
from jax import lax
from jax.experimental import pallas as pl
from jax.experimental.pallas import tpu as pltpu
from jax.sharding import PartitionSpec as P

F = 4096
WIN = 32
H = 2


def passed_along(block, axis, distance):
    devices = range(lax.axis_size(axis))
    route = [(i - distance, i) for i in devices if i - distance in devices]
    return lax.ppermute(block, axis, route)


def row_power(trace_rows):
    values = trace_rows.astype(jnp.float32)
    return jnp.sum(values * values, axis=1)


def scale_rows(trace_rows, power_total):
    factor = 1.0 / jnp.sqrt(power_total / F + 1e-06)
    return (trace_rows.astype(jnp.float32) * factor[:, None]).astype(jnp.bfloat16)


def spectra_pair(first, second):
    first_real = first[:, None, :, 0].astype(jnp.float32)
    first_imag = first[:, None, :, 1].astype(jnp.float32)
    second_real = second[None, :, :, 0].astype(jnp.float32)
    second_imag = second[None, :, :, 1].astype(jnp.float32)
    real_part = jnp.sum(first_real * second_real + first_imag * second_imag, axis=2)
    imag_part = jnp.sum(first_imag * second_real - first_real * second_imag, axis=2)
    return jnp.stack([real_part, imag_part]) / WIN


def body_by_rows(traces, row_ids):
    block_rows, _, band_bins = traces.shape
    trace_rows = traces.reshape(block_rows, 2 * band_bins)
    n_devices = lax.axis_size("chan")
    capacity = 2 * block_rows // n_devices
    trace_rows = scale_rows(trace_rows, lax.psum(row_power(trace_rows), "band"))
    owner_block = row_ids // block_rows
    member = (owner_block[:, None] == jnp.arange(n_devices)[None, :]).astype(jnp.int32)
    slot_rank = jnp.sum(member * (jnp.cumsum(member, axis=0) - 1), axis=1)
    slot_index = owner_block * capacity + slot_rank
    packing = slot_index[None, :] == jnp.arange(n_devices * capacity)[:, None]
    outgoing = jnp.dot(
        packing.astype(jnp.bfloat16), trace_rows, preferred_element_type=jnp.float32
    ).astype(jnp.bfloat16)
    label_values = (
        jnp.dot(
            packing.astype(jnp.float32),
            (row_ids + 1).astype(jnp.float32),
            precision=lax.Precision.HIGHEST,
        )
        - 1.0
    )
    sent_labels = label_values.astype(jnp.int32)
    arrived, arrived_ids = (
        lax.all_to_all(outgoing, "chan", split_axis=0, concat_axis=0, tiled=True),
        lax.all_to_all(sent_labels, "chan", split_axis=0, concat_axis=0, tiled=True),
    )
    placing = ((arrived_ids % block_rows)[None, :] == jnp.arange(block_rows)[:, None]) & (
        arrived_ids >= 0
    )[None, :]
    placed = jnp.dot(
        placing.astype(jnp.bfloat16), arrived, preferred_element_type=jnp.float32
    ).astype(jnp.bfloat16)
    chan_count = block_rows // WIN
    block_shape = (chan_count, WIN, 2, band_bins)
    local_block = placed.reshape(block_shape)
    spectra_list = [None] * (2 * H + 1)
    spectra_list[H] = spectra_pair(local_block, local_block)
    above_block = placed
    below_block = placed
    for offset in range(1, H + 1):
        above_block = passed_along(above_block, "chan", -1)
        spectra_list[H + offset] = spectra_pair(local_block, above_block.reshape(block_shape))
        below_block = passed_along(below_block, "chan", 1)
        spectra_list[H - offset] = spectra_pair(local_block, below_block.reshape(block_shape))
    return jnp.stack(spectra_list, axis=2)


LANES = 128
CH = 8
SLOTS = 2 * H + 1
MESH = pl.DeviceIdType.MESH


def exchange_kernel(
    n, nb, flat_ref, ids_ref, o_ref, recv, hot, white, placed, tmp, out, power, powers, labels,
    in_send, in_recv, out_send, out_recv, power_send, power_recv, label_send, label_recv,
):
    me = lax.axis_index("chan")
    mine = lax.axis_index("band")
    rows, width = flat_ref.shape
    band_bins = width // 2

    barrier = pltpu.get_barrier_semaphore()
    for t in range(1, n):
        pl.semaphore_signal(
            barrier, inc=1, device_id={"chan": lax.rem(me + t, n)}, device_id_type=MESH
        )
    for t in range(1, nb):
        pl.semaphore_signal(
            barrier, inc=1, device_id={"band": lax.rem(mine + t, nb)}, device_id_type=MESH
        )

    total = jnp.zeros((rows, LANES), jnp.float32)
    for i in range(width // LANES):
        value = flat_ref[:, i * LANES : (i + 1) * LANES].astype(jnp.float32)
        total += value * value
    ones = jnp.ones((8, LANES), jnp.bfloat16)
    row_sum = jnp.zeros((8, rows), jnp.float32)
    for _ in range(3):
        term = total.astype(jnp.bfloat16)
        total -= term.astype(jnp.float32)
        row_sum += lax.dot_general(
            ones, term, (((1,), (1,)), ((), ())), preferred_element_type=jnp.float32
        )
    ids = ids_ref[...]
    inside = ids & (rows - 1)
    pos = ids - inside + (ids & (WIN - 1)) * CH + lax.shift_right_logical(inside, WIN.bit_length() - 1)
    pos = jnp.broadcast_to(pos, (8, rows)).astype(jnp.float32)
    upper = lax.broadcasted_iota(jnp.int32, (8, rows), 0) < 4
    labels[0] = jnp.where(upper, row_sum, pos)

    pl.semaphore_wait(barrier, n - 1 + nb - 1)

    def power_copy(t):
        return pltpu.make_async_remote_copy(
            src_ref=power,
            dst_ref=powers.at[t],
            send_sem=power_send.at[t],
            recv_sem=power_recv.at[t],
            device_id={"band": lax.rem(mine + t, nb)},
            device_id_type=MESH,
        )

    def label_copy(t):
        return pltpu.make_async_remote_copy(
            src_ref=labels.at[0],
            dst_ref=labels.at[t],
            send_sem=label_send.at[t],
            recv_sem=label_recv.at[t],
            device_id={"chan": lax.rem(me + t, n)},
            device_id_type=MESH,
        )

    def row_copy(t, part):
        target = lax.rem(me + t, n)
        bins = pl.multiple_of(part * band_bins + target * LANES, LANES)
        return pltpu.make_async_remote_copy(
            src_ref=flat_ref.at[:, pl.ds(bins, LANES)],
            dst_ref=recv.at[t, part],
            send_sem=in_send.at[t, part],
            recv_sem=in_recv.at[t, part],
            device_id={"chan": target},
            device_id_type=MESH,
        )

    order = sorted(range(1, n), key=lambda t: -min(t, n - t))
    for t in order:
        label_copy(t).start()
    for t in order:
        for part in range(2):
            row_copy(t, part).start()

    power[0:1] = labels[0, 0:1]
    for t in reversed(order):
        label_copy(t).wait_recv()
        power[t : t + 1] = labels[t, 0:1]
    for t in range(1, nb):
        power_copy(t).start()

    def hot_chunk(b, carry):
        target = lax.broadcasted_iota(jnp.int32, (rows, rows), 0) + b * rows
        where = pl.ds(pl.multiple_of(b * rows, rows), rows)
        for t in range(n):
            place = labels[t, 4:5].astype(jnp.int32)
            hot[where, t * rows : (t + 1) * rows] = jnp.where(
                place == target, 1.0, 0.0
            ).astype(jnp.bfloat16)
        return carry

    lax.fori_loop(0, n, hot_chunk, 0)

    power_total = power[...]
    for t in range(1, nb):
        power_copy(t).wait_recv()
        power_total += powers[t]
    factor = jnp.transpose(1.0 / jnp.sqrt(power_total / F + 1e-06))

    def whiten(t, parts):
        for part in range(2):
            value = parts[part].astype(jnp.float32) * factor[:, t : t + 1]
            white[t * rows : (t + 1) * rows, part * LANES : (part + 1) * LANES] = value.astype(
                jnp.bfloat16
            )

    whiten(
        0,
        [
            flat_ref[:, pl.ds(pl.multiple_of(part * band_bins + me * LANES, LANES), LANES)]
            for part in range(2)
        ],
    )
    for t in reversed(order):
        for part in range(2):
            row_copy(t, part).wait_recv()
        whiten(t, [recv[t, 0], recv[t, 1]])

    def place_chunk(b):
        where = pl.ds(pl.multiple_of(b * rows, rows), rows)
        product = jnp.dot(hot[where, :], white[...], preferred_element_type=jnp.float32)
        placed[0, where, :] = product[:, :LANES]
        placed[1, where, :] = product[:, LANES:]

    start = me + n // 2
    for i in range(H):
        place_chunk(lax.rem(start + i, n))

    def result_copy(dest, k):
        parts = 1 if k == H else 2
        return pltpu.make_async_remote_copy(
            src_ref=out.at[dest, k, :parts],
            dst_ref=o_ref.at[me, k, :parts],
            send_sem=out_send.at[dest, k],
            recv_sem=out_recv.at[me, k],
            device_id={"chan": dest},
            device_id_type=MESH,
        )

    def deliver(dest, k):
        @pl.when(dest != me)
        def _():
            result_copy(dest, k).start()

        @pl.when(dest == me)
        def _():
            parts = 1 if k == H else 2
            o_ref[me, k, :parts] = out[dest, k, :parts]

    def pair(d, offset):
        e = d + offset

        def window(w, acc):
            first = d * rows + w * CH
            second = pl.ds(pl.multiple_of(e * rows + w * CH, CH), CH)
            yr = placed[0, second, :]
            yi = placed[1, second, :]
            new = []
            for c in range(CH):
                xr = placed[0, pl.ds(first + c, 1), :]
                xi = placed[1, pl.ds(first + c, 1), :]
                re, im = acc[2 * c], acc[2 * c + 1]
                new.append(re + (xr * yr + xi * yi))
                new.append(im + (xi * yr - xr * yi))
            return tuple(new)

        zero = jnp.zeros((CH, LANES), jnp.float32)
        acc = lax.fori_loop(0, WIN, window, (zero,) * (2 * CH), unroll=4)
        if offset == 0:
            partner = lax.broadcasted_iota(jnp.int32, (CH, LANES), 0)
            for c in range(CH):
                kept = jnp.where(partner >= c, acc[2 * c], acc[2 * c + 1])
                tmp[0, pl.ds(c * CH, CH), :] = kept * (1.0 / WIN)
            out[d, H, 0] = tmp[0].astype(jnp.bfloat16)
            deliver(d, H)
            return
        for part in range(2):
            for c in range(CH):
                tmp[part, pl.ds(c * CH, CH), :] = acc[2 * c + part] * (1.0 / WIN)
        for part in range(2):
            out[d, H + offset, part] = tmp[part].astype(jnp.bfloat16)
        deliver(d, H + offset)
        for part in range(2):
            turned = jnp.concatenate(
                [tmp[part, pl.ds(c, CH, stride=CH), :] for c in range(CH)], axis=0
            )
            turned = turned if part == 0 else -turned
            out[e, H - offset, part] = turned.astype(jnp.bfloat16)
        deliver(e, H - offset)

    def block_step(t, carry):
        pl.when(t < n - H)(lambda: place_chunk(lax.rem(start + t + H, n)))
        d = lax.rem(start + t, n)
        pair(d, 0)
        for offset in range(1, H + 1):
            pl.when(d + offset < n)(functools.partial(pair, d, offset))
        return carry

    lax.fori_loop(0, n, block_step, 0)

    for k in range(SLOTS):
        partner = me + k - H

        @pl.when((partner < 0) | (partner >= n))
        def _():
            for source in range(n):
                o_ref[source, k] = jnp.zeros(o_ref.shape[2:], o_ref.dtype)

    for t in range(1, nb):
        power_copy(t).wait_send()
    for t in range(1, n):
        label_copy(t).wait_send()
        for part in range(2):
            row_copy(t, part).wait_send()
        dest = lax.rem(me + t, n)
        source = lax.rem(me + n - t, n)
        for k in range(SLOTS):
            there = dest + k - H
            here = me + k - H

            @pl.when((there >= 0) & (there < n))
            def _():
                result_copy(dest, k).wait_send()

            @pl.when((here >= 0) & (here < n))
            def _():
                parts = 1 if k == H else 2
                pltpu.make_async_remote_copy(
                    src_ref=out.at[source, k, :parts],
                    dst_ref=o_ref.at[source, k, :parts],
                    send_sem=out_send.at[source, k],
                    recv_sem=out_recv.at[source, k],
                    device_id={"chan": source},
                    device_id_type=MESH,
                ).wait_recv()


def unpack_kernel(n, in_ref, out_ref, tmp):
    part = pl.program_id(0)
    partner = lax.broadcasted_iota(jnp.int32, (CH, LANES), 0)
    for source in range(n):
        bins = slice(source * LANES, (source + 1) * LANES)
        tmp[source] = in_ref[source, H, 0].astype(jnp.float32)
        for k in range(SLOTS):
            if k == H:
                continue
            values = in_ref[source, k, part].astype(jnp.float32)
            for c in range(CH):
                out_ref[0, c, k, :, bins] = values[c * CH : (c + 1) * CH]
        for c in range(CH):
            kept = tmp[source, pl.ds(c * CH, CH), :]
            turned = tmp[source, pl.ds(c, CH, stride=CH), :]
            real = jnp.where(partner >= c, kept, turned)
            imag = jnp.where(partner < c, kept, jnp.where(partner > c, -turned, 0.0))
            out_ref[0, c, H, :, bins] = jnp.where(part == 0, real, imag)


def body_by_bins(traces, row_ids):
    rows, _, band_bins = traces.shape
    n = lax.axis_size("chan")
    nb = lax.axis_size("band")
    flat = traces.reshape(rows, 2 * band_bins)
    vmem = pl.BlockSpec(memory_space=pltpu.VMEM)
    packed = pl.pallas_call(
        functools.partial(exchange_kernel, n, nb),
        out_shape=jax.ShapeDtypeStruct((n, SLOTS, 2, CH * CH, LANES), jnp.bfloat16),
        in_specs=[vmem, vmem],
        out_specs=vmem,
        scratch_shapes=[
            pltpu.VMEM((n, 2, rows, LANES), jnp.bfloat16),
            pltpu.VMEM((n * rows, n * rows), jnp.bfloat16),
            pltpu.VMEM((n * rows, 2 * LANES), jnp.bfloat16),
            pltpu.VMEM((2, n * rows, LANES), jnp.float32),
            pltpu.VMEM((2, CH * CH, LANES), jnp.float32),
            pltpu.VMEM((n, SLOTS, 2, CH * CH, LANES), jnp.bfloat16),
            pltpu.VMEM((n, rows), jnp.float32),
            pltpu.VMEM((nb, n, rows), jnp.float32),
            pltpu.VMEM((n, 8, rows), jnp.float32),
            pltpu.SemaphoreType.DMA((n, 2)),
            pltpu.SemaphoreType.DMA((n, 2)),
            pltpu.SemaphoreType.DMA((n, SLOTS)),
            pltpu.SemaphoreType.DMA((n, SLOTS)),
            pltpu.SemaphoreType.DMA((nb,)),
            pltpu.SemaphoreType.DMA((nb,)),
            pltpu.SemaphoreType.DMA((n,)),
            pltpu.SemaphoreType.DMA((n,)),
        ],
        compiler_params=pltpu.CompilerParams(
            collective_id=0, has_side_effects=True, vmem_limit_bytes=40 * 2**20
        ),
    )(flat, row_ids.reshape(1, rows))
    return pl.pallas_call(
        functools.partial(unpack_kernel, n),
        grid=(2,),
        out_shape=jax.ShapeDtypeStruct((2, rows // WIN, SLOTS, CH, band_bins), jnp.float32),
        in_specs=[pl.BlockSpec((n, SLOTS, 2, CH * CH, LANES), lambda p: (0, 0, 0, 0, 0))],
        out_specs=pl.BlockSpec((1, rows // WIN, SLOTS, CH, band_bins), lambda p: (p, 0, 0, 0, 0)),
        scratch_shapes=[pltpu.VMEM((n, CH * CH, LANES), jnp.float32)],
        compiler_params=pltpu.CompilerParams(vmem_limit_bytes=40 * 2**20),
    )(packed)


def body(traces, row_ids):
    rows, _, band_bins = traces.shape
    by_bins = band_bins == lax.axis_size("chan") * LANES and rows == CH * WIN
    return (body_by_bins if by_bins else body_by_rows)(traces, row_ids)


def solution(mesh):
    in_specs = (P("chan", None, "band"), P("chan"))
    out_specs = P(None, "chan", None, None, "band")
    return jax.shard_map(body, mesh=mesh, in_specs=in_specs, out_specs=out_specs, check_vma=False)
```

```python
import functools

import jax
import jax.numpy as jnp
from jax import lax
from jax.experimental import pallas as pl
from jax.experimental.pallas import tpu as pltpu
from jax.sharding import PartitionSpec as P

F = 4096
WIN = 32
H = 2


def passed_along(block, axis, distance):
    devices = range(lax.axis_size(axis))
    route = [(i - distance, i) for i in devices if i - distance in devices]
    return lax.ppermute(block, axis, route)


def row_power(trace_rows):
    values = trace_rows.astype(jnp.float32)
    return jnp.sum(values * values, axis=1)


def scale_rows(trace_rows, power_total):
    factor = 1.0 / jnp.sqrt(power_total / F + 1e-06)
    return (trace_rows.astype(jnp.float32) * factor[:, None]).astype(jnp.bfloat16)


def spectra_pair(first, second):
    first_real = first[:, None, :, 0].astype(jnp.float32)
    first_imag = first[:, None, :, 1].astype(jnp.float32)
    second_real = second[None, :, :, 0].astype(jnp.float32)
    second_imag = second[None, :, :, 1].astype(jnp.float32)
    real_part = jnp.sum(first_real * second_real + first_imag * second_imag, axis=2)
    imag_part = jnp.sum(first_imag * second_real - first_real * second_imag, axis=2)
    return jnp.stack([real_part, imag_part]) / WIN


def body_by_rows(traces, row_ids):
    block_rows, _, band_bins = traces.shape
    trace_rows = traces.reshape(block_rows, 2 * band_bins)
    n_devices = lax.axis_size("chan")
    capacity = 2 * block_rows // n_devices
    trace_rows = scale_rows(trace_rows, lax.psum(row_power(trace_rows), "band"))
    owner_block = row_ids // block_rows
    member = (owner_block[:, None] == jnp.arange(n_devices)[None, :]).astype(jnp.int32)
    slot_rank = jnp.sum(member * (jnp.cumsum(member, axis=0) - 1), axis=1)
    slot_index = owner_block * capacity + slot_rank
    packing = slot_index[None, :] == jnp.arange(n_devices * capacity)[:, None]
    outgoing = jnp.dot(
        packing.astype(jnp.bfloat16), trace_rows, preferred_element_type=jnp.float32
    ).astype(jnp.bfloat16)
    label_values = (
        jnp.dot(
            packing.astype(jnp.float32),
            (row_ids + 1).astype(jnp.float32),
            precision=lax.Precision.HIGHEST,
        )
        - 1.0
    )
    sent_labels = label_values.astype(jnp.int32)
    arrived, arrived_ids = (
        lax.all_to_all(outgoing, "chan", split_axis=0, concat_axis=0, tiled=True),
        lax.all_to_all(sent_labels, "chan", split_axis=0, concat_axis=0, tiled=True),
    )
    placing = ((arrived_ids % block_rows)[None, :] == jnp.arange(block_rows)[:, None]) & (
        arrived_ids >= 0
    )[None, :]
    placed = jnp.dot(
        placing.astype(jnp.bfloat16), arrived, preferred_element_type=jnp.float32
    ).astype(jnp.bfloat16)
    chan_count = block_rows // WIN
    block_shape = (chan_count, WIN, 2, band_bins)
    local_block = placed.reshape(block_shape)
    spectra_list = [None] * (2 * H + 1)
    spectra_list[H] = spectra_pair(local_block, local_block)
    above_block = placed
    below_block = placed
    for offset in range(1, H + 1):
        above_block = passed_along(above_block, "chan", -1)
        spectra_list[H + offset] = spectra_pair(local_block, above_block.reshape(block_shape))
        below_block = passed_along(below_block, "chan", 1)
        spectra_list[H - offset] = spectra_pair(local_block, below_block.reshape(block_shape))
    return jnp.stack(spectra_list, axis=2)


LANES = 128
CH = 8
SLOTS = 2 * H + 1
MESH = pl.DeviceIdType.MESH


def exchange_kernel(
    n, nb, flat_ref, ids_ref, o_ref, recv, hot, white, placed, tmp, out, power, powers, labels,
    in_send, in_recv, out_send, out_recv, power_send, power_recv, label_send, label_recv,
):
    me = lax.axis_index("chan")
    mine = lax.axis_index("band")
    rows, width = flat_ref.shape
    band_bins = width // 2

    barrier = pltpu.get_barrier_semaphore()
    for t in range(1, n):
        pl.semaphore_signal(
            barrier, inc=1, device_id={"chan": lax.rem(me + t, n)}, device_id_type=MESH
        )
    for t in range(1, nb):
        pl.semaphore_signal(
            barrier, inc=1, device_id={"band": lax.rem(mine + t, nb)}, device_id_type=MESH
        )

    total = jnp.zeros((rows, LANES), jnp.float32)
    for i in range(width // LANES):
        value = flat_ref[:, i * LANES : (i + 1) * LANES].astype(jnp.float32)
        total += value * value
    ones = jnp.ones((8, LANES), jnp.bfloat16)
    row_sum = jnp.zeros((8, rows), jnp.float32)
    for _ in range(3):
        term = total.astype(jnp.bfloat16)
        total -= term.astype(jnp.float32)
        row_sum += lax.dot_general(
            ones, term, (((1,), (1,)), ((), ())), preferred_element_type=jnp.float32
        )
    ids = ids_ref[...]
    inside = ids & (rows - 1)
    pos = ids - inside + (ids & (WIN - 1)) * CH + lax.shift_right_logical(inside, WIN.bit_length() - 1)
    pos = jnp.broadcast_to(pos, (8, rows)).astype(jnp.float32)
    upper = lax.broadcasted_iota(jnp.int32, (8, rows), 0) < 4
    labels[0] = jnp.where(upper, row_sum, pos)

    pl.semaphore_wait(barrier, n - 1 + nb - 1)

    def power_copy(t):
        return pltpu.make_async_remote_copy(
            src_ref=power,
            dst_ref=powers.at[t],
            send_sem=power_send.at[t],
            recv_sem=power_recv.at[t],
            device_id={"band": lax.rem(mine + t, nb)},
            device_id_type=MESH,
        )

    def label_copy(t):
        return pltpu.make_async_remote_copy(
            src_ref=labels.at[0],
            dst_ref=labels.at[t],
            send_sem=label_send.at[t],
            recv_sem=label_recv.at[t],
            device_id={"chan": lax.rem(me + t, n)},
            device_id_type=MESH,
        )

    def row_copy(t, part):
        target = lax.rem(me + t, n)
        bins = pl.multiple_of(part * band_bins + target * LANES, LANES)
        return pltpu.make_async_remote_copy(
            src_ref=flat_ref.at[:, pl.ds(bins, LANES)],
            dst_ref=recv.at[t, part],
            send_sem=in_send.at[t, part],
            recv_sem=in_recv.at[t, part],
            device_id={"chan": target},
            device_id_type=MESH,
        )

    order = sorted(range(1, n), key=lambda t: min(t, n - t))
    for t in order:
        label_copy(t).start()
    for t in order:
        for part in range(2):
            row_copy(t, part).start()

    power[0:1] = labels[0, 0:1]
    for t in reversed(order):
        label_copy(t).wait_recv()
        power[t : t + 1] = labels[t, 0:1]
    for t in range(1, nb):
        power_copy(t).start()

    def hot_chunk(b, carry):
        target = lax.broadcasted_iota(jnp.int32, (rows, rows), 0) + b * rows
        where = pl.ds(pl.multiple_of(b * rows, rows), rows)
        for t in range(n):
            place = labels[t, 4:5].astype(jnp.int32)
            hot[where, t * rows : (t + 1) * rows] = jnp.where(
                place == target, 1.0, 0.0
            ).astype(jnp.bfloat16)
        return carry

    lax.fori_loop(0, n, hot_chunk, 0)

    power_total = power[...]
    for t in range(1, nb):
        power_copy(t).wait_recv()
        power_total += powers[t]
    factor = jnp.transpose(1.0 / jnp.sqrt(power_total / F + 1e-06))

    def whiten(t, parts):
        for part in range(2):
            value = parts[part].astype(jnp.float32) * factor[:, t : t + 1]
            white[t * rows : (t + 1) * rows, part * LANES : (part + 1) * LANES] = value.astype(
                jnp.bfloat16
            )

    whiten(
        0,
        [
            flat_ref[:, pl.ds(pl.multiple_of(part * band_bins + me * LANES, LANES), LANES)]
            for part in range(2)
        ],
    )
    for t in reversed(order):
        for part in range(2):
            row_copy(t, part).wait_recv()
        whiten(t, [recv[t, 0], recv[t, 1]])

    def place_chunk(b):
        where = pl.ds(pl.multiple_of(b * rows, rows), rows)
        product = jnp.dot(hot[where, :], white[...], preferred_element_type=jnp.float32)
        placed[0, where, :] = product[:, :LANES]
        placed[1, where, :] = product[:, LANES:]

    start = me + n // 2
    for i in range(H):
        place_chunk(lax.rem(start + i, n))

    def result_copy(dest, k):
        parts = 1 if k == H else 2
        return pltpu.make_async_remote_copy(
            src_ref=out.at[dest, k, :parts],
            dst_ref=o_ref.at[me, k, :parts],
            send_sem=out_send.at[dest, k],
            recv_sem=out_recv.at[me, k],
            device_id={"chan": dest},
            device_id_type=MESH,
        )

    def deliver(dest, k):
        @pl.when(dest != me)
        def _():
            result_copy(dest, k).start()

        @pl.when(dest == me)
        def _():
            parts = 1 if k == H else 2
            o_ref[me, k, :parts] = out[dest, k, :parts]

    def pair(d, offset):
        e = d + offset

        def window(w, acc):
            first = d * rows + w * CH
            second = pl.ds(pl.multiple_of(e * rows + w * CH, CH), CH)
            yr = placed[0, second, :]
            yi = placed[1, second, :]
            new = []
            for c in range(CH):
                xr = placed[0, pl.ds(first + c, 1), :]
                xi = placed[1, pl.ds(first + c, 1), :]
                re, im = acc[2 * c], acc[2 * c + 1]
                new.append(re + (xr * yr + xi * yi))
                new.append(im + (xi * yr - xr * yi))
            return tuple(new)

        zero = jnp.zeros((CH, LANES), jnp.float32)
        acc = lax.fori_loop(0, WIN, window, (zero,) * (2 * CH), unroll=4)
        if offset == 0:
            partner = lax.broadcasted_iota(jnp.int32, (CH, LANES), 0)
            for c in range(CH):
                kept = jnp.where(partner >= c, acc[2 * c], acc[2 * c + 1])
                tmp[0, pl.ds(c * CH, CH), :] = kept * (1.0 / WIN)
            out[d, H, 0] = tmp[0].astype(jnp.bfloat16)
            deliver(d, H)
            return
        for part in range(2):
            for c in range(CH):
                tmp[part, pl.ds(c * CH, CH), :] = acc[2 * c + part] * (1.0 / WIN)
        for part in range(2):
            out[d, H + offset, part] = tmp[part].astype(jnp.bfloat16)
        deliver(d, H + offset)
        for part in range(2):
            turned = jnp.concatenate(
                [tmp[part, pl.ds(c, CH, stride=CH), :] for c in range(CH)], axis=0
            )
            turned = turned if part == 0 else -turned
            out[e, H - offset, part] = turned.astype(jnp.bfloat16)
        deliver(e, H - offset)

    def block_step(t, carry):
        pl.when(t < n - H)(lambda: place_chunk(lax.rem(start + t + H, n)))
        d = lax.rem(start + t, n)
        pair(d, 0)
        for offset in range(1, H + 1):
            pl.when(d + offset < n)(functools.partial(pair, d, offset))
        return carry

    lax.fori_loop(0, n, block_step, 0)

    for k in range(SLOTS):
        partner = me + k - H

        @pl.when((partner < 0) | (partner >= n))
        def _():
            for source in range(n):
                o_ref[source, k] = jnp.zeros(o_ref.shape[2:], o_ref.dtype)

    for t in range(1, nb):
        power_copy(t).wait_send()
    for t in range(1, n):
        label_copy(t).wait_send()
        for part in range(2):
            row_copy(t, part).wait_send()
        dest = lax.rem(me + t, n)
        source = lax.rem(me + n - t, n)
        for k in range(SLOTS):
            there = dest + k - H
            here = me + k - H

            @pl.when((there >= 0) & (there < n))
            def _():
                result_copy(dest, k).wait_send()

            @pl.when((here >= 0) & (here < n))
            def _():
                parts = 1 if k == H else 2
                pltpu.make_async_remote_copy(
                    src_ref=out.at[source, k, :parts],
                    dst_ref=o_ref.at[source, k, :parts],
                    send_sem=out_send.at[source, k],
                    recv_sem=out_recv.at[source, k],
                    device_id={"chan": source},
                    device_id_type=MESH,
                ).wait_recv()


def unpack_kernel(n, in_ref, out_ref, tmp):
    part = pl.program_id(0)
    partner = lax.broadcasted_iota(jnp.int32, (CH, LANES), 0)
    for source in range(n):
        bins = slice(source * LANES, (source + 1) * LANES)
        tmp[source] = in_ref[source, H, 0].astype(jnp.float32)
        for k in range(SLOTS):
            if k == H:
                continue
            values = in_ref[source, k, part].astype(jnp.float32)
            for c in range(CH):
                out_ref[0, c, k, :, bins] = values[c * CH : (c + 1) * CH]
        for c in range(CH):
            kept = tmp[source, pl.ds(c * CH, CH), :]
            turned = tmp[source, pl.ds(c, CH, stride=CH), :]
            real = jnp.where(partner >= c, kept, turned)
            imag = jnp.where(partner < c, kept, jnp.where(partner > c, -turned, 0.0))
            out_ref[0, c, H, :, bins] = jnp.where(part == 0, real, imag)


def body_by_bins(traces, row_ids):
    rows, _, band_bins = traces.shape
    n = lax.axis_size("chan")
    nb = lax.axis_size("band")
    flat = traces.reshape(rows, 2 * band_bins)
    vmem = pl.BlockSpec(memory_space=pltpu.VMEM)
    packed = pl.pallas_call(
        functools.partial(exchange_kernel, n, nb),
        out_shape=jax.ShapeDtypeStruct((n, SLOTS, 2, CH * CH, LANES), jnp.bfloat16),
        in_specs=[vmem, vmem],
        out_specs=vmem,
        scratch_shapes=[
            pltpu.VMEM((n, 2, rows, LANES), jnp.bfloat16),
            pltpu.VMEM((n * rows, n * rows), jnp.bfloat16),
            pltpu.VMEM((n * rows, 2 * LANES), jnp.bfloat16),
            pltpu.VMEM((2, n * rows, LANES), jnp.float32),
            pltpu.VMEM((2, CH * CH, LANES), jnp.float32),
            pltpu.VMEM((n, SLOTS, 2, CH * CH, LANES), jnp.bfloat16),
            pltpu.VMEM((n, rows), jnp.float32),
            pltpu.VMEM((nb, n, rows), jnp.float32),
            pltpu.VMEM((n, 8, rows), jnp.float32),
            pltpu.SemaphoreType.DMA((n, 2)),
            pltpu.SemaphoreType.DMA((n, 2)),
            pltpu.SemaphoreType.DMA((n, SLOTS)),
            pltpu.SemaphoreType.DMA((n, SLOTS)),
            pltpu.SemaphoreType.DMA((nb,)),
            pltpu.SemaphoreType.DMA((nb,)),
            pltpu.SemaphoreType.DMA((n,)),
            pltpu.SemaphoreType.DMA((n,)),
        ],
        compiler_params=pltpu.CompilerParams(
            collective_id=0, has_side_effects=True, vmem_limit_bytes=40 * 2**20
        ),
    )(flat, row_ids.reshape(1, rows))
    return pl.pallas_call(
        functools.partial(unpack_kernel, n),
        grid=(2,),
        out_shape=jax.ShapeDtypeStruct((2, rows // WIN, SLOTS, CH, band_bins), jnp.float32),
        in_specs=[pl.BlockSpec((n, SLOTS, 2, CH * CH, LANES), lambda p: (0, 0, 0, 0, 0))],
        out_specs=pl.BlockSpec((1, rows // WIN, SLOTS, CH, band_bins), lambda p: (p, 0, 0, 0, 0)),
        scratch_shapes=[pltpu.VMEM((n, CH * CH, LANES), jnp.float32)],
        compiler_params=pltpu.CompilerParams(vmem_limit_bytes=40 * 2**20),
    )(packed)


def body(traces, row_ids):
    rows, _, band_bins = traces.shape
    by_bins = band_bins == lax.axis_size("chan") * LANES and rows == CH * WIN
    return (body_by_bins if by_bins else body_by_rows)(traces, row_ids)


def solution(mesh):
    in_specs = (P("chan", None, "band"), P("chan"))
    out_specs = P(None, "chan", None, None, "band")
    return jax.shard_map(body, mesh=mesh, in_specs=in_specs, out_specs=out_specs, check_vma=False)
```
